32 devices in a mesh: section: 2 (over x), owner: 4 (over z), context: 4 (over y, core).
Axes of the slice: x: 2, y: 2, z: 4, core: 2. Of those that a mesh axis runs over, the one named last changes fastest.
Arguments:
- x_attn: bfloat16 [16384, 8192], P(('section', 'context'), 'owner'), parts along dimension 0, may hold values from -6 to 6
- x_mlp: bfloat16 [16384, 8192], P(('section', 'context'), 'owner'), parts along dimension 0, may hold values from -6 to 6
- x_down: bfloat16 [16384, 29568], P(('section', 'context'), 'owner'), parts along dimension 0, may hold values from -6 to 6
- omega_attn: bfloat16 [16384, 256], P(('section', 'owner')), parts along dimension 0, may hold values from -6 to 6
- omega_mlp: bfloat16 [16384, 256], P(('section', 'owner')), parts along dimension 0, may hold values from -6 to 6
- omega_down: bfloat16 [59136, 256], P(('section', 'owner')), parts along dimension 0, may hold values from -6 to 6
- basis_attn: bfloat16 [16384, 256], P(('section', 'owner')), parts along dimension 0, may hold values from -1 to 1
- basis_mlp: bfloat16 [16384, 256], P(('section', 'owner')), parts along dimension 0, may hold values from -1 to 1
- basis_down: bfloat16 [59136, 256], P(('section', 'owner')), parts along dimension 0, may hold values from -1 to 1
- eig_attn: float32 [512], P('section'), parts along dimension 0, may hold values from 2 to 20
- eig_mlp: float32 [512], P('section'), parts along dimension 0, may hold values from 2 to 20
- eig_down: float32 [512], P('section'), parts along dimension 0, may hold values from 2 to 20
Outputs:
- sketch_attn: float32 [16384, 256], P(('section', 'owner', 'context')), parts along dimension 0
- sketch_mlp: float32 [16384, 256], P(('section', 'owner', 'context')), parts along dimension 0
- sketch_down: float32 [59136, 256], P(('section', 'owner', 'context')), parts along dimension 0
The draws below stay inside these ranges and needn't reach their ends.
There are 2 independent parts, one for each index of `section`. The reference program is written for one: setup_inputs(seed, part) draws one part's arguments, and reference() takes and returns one part's arrays. A program takes and returns all parts, laid end to end along the dimension named above; each array names one. Nothing has to cross between parts.
All inputs are finite; a program needn't handle non-finite values.
Results may differ from the reference program's by a relative error of at most 0.0003.
Values may be sent and summed in bfloat16 or wider, within the bound.
No kernel may reach another device: no remote copies, remote signals or barrier semaphores. Data moves between devices by JAX's collectives and lax.ppermute only.
A program may use at most 128 MiB of HBM per device.

```python
import math
import jax
import jax.numpy as jnp
from jax import lax

D = 8192
FF = 29568
R = 256
TOKENS = 8192


def drawn_draw(key, label, rows, cols, scale):
    own_key = jax.random.fold_in(key, label)
    values = jnp.clip(jax.random.normal(jax.random.fold_in(own_key, 13), (rows, cols), jnp.float32), -6.0, 6.0)
    return (values * scale).astype(jnp.bfloat16)


def draw_x_attn(key, part):
    return drawn_draw(key, 1, TOKENS, D, 1.0)


def draw_x_mlp(key, part):
    return drawn_draw(key, 2, TOKENS, D, 1.0)


def draw_x_down(key, part):
    return drawn_draw(key, 3, TOKENS, FF, 1.0)


def draw_omega_attn(key, part):
    return drawn_draw(key, 4, D, R, 1.0)


def draw_omega_mlp(key, part):
    return drawn_draw(key, 5, D, R, 1.0)


def draw_omega_down(key, part):
    return drawn_draw(key, 6, FF, R, 1.0)


def draw_basis_attn(key, part):
    return drawn_draw(key, 7, D, R, 1.0 / D ** 0.5)


def draw_basis_mlp(key, part):
    return drawn_draw(key, 8, D, R, 1.0 / D ** 0.5)


def draw_basis_down(key, part):
    return drawn_draw(key, 9, FF, R, 1.0 / FF ** 0.5)


def setup_inputs(seed: int = 0, part: int = 0) -> dict:
    arg_keys = jax.random.split(jax.random.key(seed), 13)
    own_keys = jax.random.split(jax.random.fold_in(arg_keys[12], part), 13)
    x_attn = draw_x_attn(jax.random.fold_in(jax.random.fold_in(arg_keys[12], part), 71), part)
    x_mlp = draw_x_mlp(jax.random.fold_in(jax.random.fold_in(arg_keys[12], part), 71), part)
    x_down = draw_x_down(jax.random.fold_in(jax.random.fold_in(arg_keys[12], part), 71), part)
    omega_attn = draw_omega_attn(jax.random.fold_in(jax.random.fold_in(arg_keys[12], part), 71), part)
    omega_mlp = draw_omega_mlp(jax.random.fold_in(jax.random.fold_in(arg_keys[12], part), 71), part)
    omega_down = draw_omega_down(jax.random.fold_in(jax.random.fold_in(arg_keys[12], part), 71), part)
    basis_attn = draw_basis_attn(jax.random.fold_in(jax.random.fold_in(arg_keys[12], part), 71), part)
    basis_mlp = draw_basis_mlp(jax.random.fold_in(jax.random.fold_in(arg_keys[12], part), 71), part)
    basis_down = draw_basis_down(jax.random.fold_in(jax.random.fold_in(arg_keys[12], part), 71), part)
    eig_attn = jnp.clip(jnp.exp(jax.random.uniform(own_keys[9], (R,), jnp.float32, math.log(2.0), math.log(20.0))), 2.0, 20.0)
    eig_mlp = jnp.clip(jnp.exp(jax.random.uniform(own_keys[10], (R,), jnp.float32, math.log(2.0), math.log(20.0))), 2.0, 20.0)
    eig_down = jnp.clip(jnp.exp(jax.random.uniform(own_keys[11], (R,), jnp.float32, math.log(2.0), math.log(20.0))), 2.0, 20.0)
    return {"x_attn": x_attn, "x_mlp": x_mlp, "x_down": x_down, "omega_attn": omega_attn, "omega_mlp": omega_mlp, "omega_down": omega_down, "basis_attn": basis_attn, "basis_mlp": basis_mlp, "basis_down": basis_down, "eig_attn": eig_attn, "eig_mlp": eig_mlp, "eig_down": eig_down}


def one_factor(inputs, omega, basis, eigen, total):
    probe = jnp.dot(inputs, omega, preferred_element_type=jnp.float32).astype(jnp.bfloat16)
    core = jnp.dot(basis.T, omega, preferred_element_type=jnp.float32)
    data = jnp.dot(inputs.T, probe, preferred_element_type=jnp.float32)
    weighted = eigen[:, None] * core
    prior = jnp.dot(basis.astype(jnp.float32), weighted, precision=lax.Precision.HIGHEST)
    return 0.9 * prior + (0.1 / total) * data


def reference(x_attn, x_mlp, x_down, omega_attn, omega_mlp, omega_down, basis_attn, basis_mlp, basis_down, eig_attn, eig_mlp, eig_down):
    total = x_attn.shape[0]
    first = one_factor(x_attn, omega_attn, basis_attn, eig_attn, total)
    second = one_factor(x_mlp, omega_mlp, basis_mlp, eig_mlp, total)
    third = one_factor(x_down, omega_down, basis_down, eig_down, total)
    return (first, second, third)
```

```python
import functools

import jax
import jax.numpy as jnp
from jax import lax
from jax.experimental import pallas as pl
from jax.experimental.pallas import tpu as pltpu
from jax.sharding import PartitionSpec as P

INWARD = ((0, 1), (3, 2))
ACROSS = ((1, 2), (2, 1))
OUTWARD = ((1, 0), (2, 3))
PAIRED = ((0, 1), (1, 0), (2, 3), (3, 2))
SKIPPED = ((0, 2), (2, 0), (1, 3), (3, 1))
CHUNKS = 2
CARRIER = 2
MIB = 1024 * 1024
FIRST = (((0,), (0,)), ((), ()))
ANYWHERE = pl.BlockSpec(memory_space=pl.ANY)


def token_contract(inputs, probe):
    return lax.dot_general(inputs, probe, FIRST, preferred_element_type=jnp.float32)


def prior_rows(basis, eigen, core):
    rows = basis.shape[0] // lax.axis_size("context")
    picked = lax.dynamic_slice_in_dim(basis, lax.axis_index("context") * rows, rows, 0)
    weighted = eigen[:, None] * core
    return 0.9 * jnp.dot(picked.astype(jnp.float32), weighted, precision=lax.Precision.HIGHEST)


def core_total(bases, omegas):
    size = lax.axis_size("context")
    rank = omegas[0].shape[1]
    share = rank // size
    start = lax.axis_index("context") * share
    mine = [
        token_contract(lax.dynamic_slice_in_dim(b, start, share, 1), w)
        for b, w in zip(bases, omegas)
    ]
    summed = lax.psum(jnp.concatenate(mine, 0), "owner")
    whole = lax.all_gather(summed, "context", axis=0)
    whole = whole.reshape(size, len(bases), share, rank)
    return [whole[:, k].reshape(rank, rank) for k in range(len(bases))]


class Order:
    def __init__(self):
        self.last = ()

    def call(self, kernel, operands, out, after=(), vmem=8 * MIB, **rest):
        held = (*self.last, *after)
        count = len(operands)

        def body(*refs):
            kernel(*refs[:count], *refs[count + len(held) :])

        specs = rest.pop("in_specs", [pl.BlockSpec(memory_space=pltpu.VMEM)] * count)
        result = pl.pallas_call(
            body,
            out_shape=out,
            in_specs=[*specs, *[ANYWHERE] * len(held)],
            cost_estimate=pl.CostEstimate(flops=1000, bytes_accessed=1000, transcendentals=0),
            compiler_params=pltpu.CompilerParams(vmem_limit_bytes=vmem),
            **rest,
        )(*operands, *held)
        self.last = (result[-1] if isinstance(result, (tuple, list)) else result,)
        return result


def probe_rows(order, inputs, omega, start, rows, turned):
    tile = 512
    rank = omega.shape[1]
    first = start // tile

    def kernel(x, w, out):
        if turned:
            out[...] = token_contract(x[...], w[...])
        else:
            out[...] = jnp.dot(x[...], w[...], preferred_element_type=jnp.float32)

    depth = omega.shape[0]
    if turned:
        spec = pl.BlockSpec((depth, tile), lambda i: (0, first + i))
    else:
        spec = pl.BlockSpec((tile, depth), lambda i: (first + i, 0))
    return order.call(
        kernel,
        (inputs, omega),
        jax.ShapeDtypeStruct((rows, rank), jnp.float32),
        vmem=44 * MIB,
        grid=(rows // tile,),
        in_specs=[spec, pl.BlockSpec((depth, rank), lambda i: (0, 0))],
        out_specs=pl.BlockSpec((tile, rank), lambda i: (i, 0)),
    )


def paired(order, partial, arrived, after):
    half = partial.shape[0] // 2

    def kernel(mine, theirs, kept, given):
        here = lax.select(lax.axis_index("owner") < 2, 0, half)
        near = pl.ds(pl.multiple_of(here, half), half)
        away = pl.ds(pl.multiple_of(half - here, half), half)
        given[...] = mine[away, :] + theirs[away, :]
        kept[...] = mine[near, :] + theirs[near, :]

    shape = jax.ShapeDtypeStruct((half, partial.shape[1]), jnp.float32)
    return order.call(kernel, (partial, arrived), (shape, shape), after)


def rounded(order, kept, arrived, exact):
    rows, rank = kept.shape
    plain = rows - exact

    def kernel(mine, theirs, out):
        total = mine[...] + theirs[...]
        out[:plain, :] = total[:plain].astype(jnp.bfloat16)
        rest = total[plain:]
        for i in range(3 if exact else 0):
            term = rest.astype(jnp.bfloat16)
            out[plain + i * exact : plain + (i + 1) * exact, :] = term
            rest = rest - term.astype(jnp.float32)

    shape = jax.ShapeDtypeStruct((plain + 3 * exact, rank), jnp.bfloat16)
    return order.call(kernel, (kept, arrived), shape)


def data_rows(order, inputs, probe, turned):
    features = inputs.shape[0] if turned else inputs.shape[1]
    tokens, rank = probe.shape
    tile = features // 4 if turned else features // 2

    def kernel(x, p, out):
        if turned:
            out[...] = jnp.dot(x[...], p[...], preferred_element_type=jnp.float32)
        else:
            out[...] = token_contract(x[...], p[...])

    if turned:
        tile = -(-features // 64) * 16
        spec = pl.BlockSpec((tile, tokens), lambda i: (i, 0))
    else:
        spec = pl.BlockSpec((tokens, tile), lambda i: (0, i))
    return order.call(
        kernel,
        (inputs, probe),
        jax.ShapeDtypeStruct((features, rank), jnp.float32),
        vmem=44 * MIB,
        grid=(pl.cdiv(features, tile),),
        in_specs=[spec, pl.BlockSpec((tokens, rank), lambda i: (0, 0))],
        out_specs=pl.BlockSpec((tile, rank), lambda i: (i, 0)),
    )


def halves(data, other):
    quarters = data.reshape(2, 2, data.shape[0] // 4, data.shape[1])
    return lax.dynamic_index_in_dim(quarters, other, 1, keepdims=False)


def core_summed(order, kept, arrived):
    def kernel(mine, theirs, stays, given):
        high = lax.select(lax.axis_index("context") >= 2, 1, 0)
        given[...] = mine[1 - high] + theirs[1 - high]
        stays[...] = mine[high] + theirs[high]

    shape = jax.ShapeDtypeStruct(kept.shape[1:], jnp.float32)
    return order.call(kernel, (kept, arrived), (shape, shape))


def finished(order, stays, arrived, prior, scale):
    def kernel(mine, theirs, before, out):
        out[...] = before[...] + scale * (mine[...] + theirs[...])

    return order.call(
        kernel, (stays, arrived, prior), jax.ShapeDtypeStruct(stays.shape, jnp.float32)
    )


def assembled(order, near, far):
    half = near.shape[0]

    def kernel(here, away, out):
        place = lax.select(lax.axis_index("owner") < 2, 0, half)
        out[pl.ds(pl.multiple_of(place, half), half), :] = here[...]
        out[pl.ds(pl.multiple_of(half - place, half), half), :] = away[...]

    shape = jax.ShapeDtypeStruct((2 * half, near.shape[1]), near.dtype)
    return order.call(kernel, (near, far), shape)


def core_parts(order, bases, omegas):
    rank = omegas[0].shape[1]
    share = rank // lax.axis_size("context")
    count = len(bases)

    def kernel(*refs):
        out, product = refs[-2:]
        start = pl.multiple_of(lax.axis_index("context") * share, share)
        for k in range(count):
            product[...] = token_contract(refs[k][...], refs[count + k][...])
            out[k * share : (k + 1) * share, :] = product[pl.ds(start, share), :]

    shape = jax.ShapeDtypeStruct((count * share, rank), jnp.float32)
    scratch = [pltpu.VMEM((rank, rank), jnp.float32)]
    return order.call(kernel, (*bases, *omegas), shape, vmem=44 * MIB, scratch_shapes=scratch)


def lines_of_four(inputs, omegas, bases, eigens, scale):
    place = lax.axis_index("owner")
    inner = (place == 1) | (place == 2)
    turned = [x.shape[1] % 128 != 0 for x in inputs]
    inputs = [x.T if t else x for x, t in zip(inputs, turned)]
    order = Order()
    jobs = [(k, c) for k in (2, 0, 1) for c in range(CHUNKS)]
    count = len(jobs)
    partial, inward, pair, across, near, far, probe, outward = ([None] * count for _ in range(8))
    state = [None] * 3
    results = [None] * 3

    def multiply(i):
        k, c = jobs[i]
        rows = inputs[k].shape[1 if turned[k] else 0] // CHUNKS
        partial[i] = probe_rows(order, inputs[k], omegas[k], c * rows, rows, turned[k])
        if i == CARRIER:
            half, part = rows // 2, cores.shape[0] // 2
            pieces = [partial[i][:half], cores[:part], partial[i][half:], cores[part:]]
            partial[i] = jnp.concatenate(pieces, 0)
        inward[i] = lax.ppermute(partial[i], "owner", INWARD)

    def add_pair(i, after=()):
        kept, given = paired(order, partial[i], inward[i], after)
        pair[i] = kept
        across[i] = lax.ppermute(given, "owner", ACROSS)

    def add_across(i):
        exact = cores.shape[0] // 2 if i == CARRIER else 0
        near[i] = rounded(order, pair[i], across[i], exact)
        far[i] = lax.ppermute(near[i], "owner", ACROSS)

    def assemble(i):
        probe[i] = assembled(order, near[i], far[i])
        outward[i] = lax.ppermute(probe[i], "owner", OUTWARD)

    def carried(i):
        whole = lax.select(inner, probe[i], outward[i])
        if i != CARRIER:
            return whole, None
        part = cores.shape[0] // 2
        half = whole.shape[0] // 2
        plain = half - 3 * part
        terms = [
            whole[h * half + plain :][: 3 * part].reshape(3, part, -1).astype(jnp.float32)
            for h in range(2)
        ]
        total = jnp.concatenate([t[0] + (t[1] + t[2]) for t in terms], 0)
        return jnp.concatenate([whole[:plain], whole[half : half + plain]], 0), total

    def contract(k):
        pieces = [chunk[i] for i in range(count) if jobs[i][0] == k]
        data = data_rows(order, inputs[k], jnp.concatenate(pieces, 0), turned[k])
        if turned[k]:
            state[k] = lax.psum_scatter(data, "context", scatter_dimension=0, tiled=True)
        else:
            core = lax.axis_index("context") % 2
            state[k] = halves(data, core), lax.ppermute(halves(data, 1 - core), "context", PAIRED)

    def add_cores(k):
        stays, given = core_summed(order, *state[k])
        state[k] = stays, lax.ppermute(given, "context", SKIPPED)

    def finish(k):
        results[k] = finished(order, *state[k], priors[k], scale)

    rank = omegas[0].shape[1]
    chunk = [None] * count
    multiply(0)
    multiply(1)
    cores = core_parts(order, bases, omegas)
    priors = ()
    for i in range(count):
        after = () if i < 2 else (outward[i - 2],)
        add_pair(i, (*after, *priors) if i == CARRIER + 3 else after)
        if i + 2 < count:
            multiply(i + 2)
        if i > 1:
            chunk[i - 2], total = carried(i - 2)
            if i - 2 == CARRIER:
                total = lax.all_gather(total, "context", axis=0).reshape(4, 3, rank // 4, rank)
                total = [total[:, k].reshape(rank, rank) for k in range(3)]
                priors = [prior_rows(b, e, c) for b, e, c in zip(bases, eigens, total)]
        if i > 0:
            assemble(i - 1)
        if i > 1 and jobs[i - 2][1] == CHUNKS - 1:
            contract(jobs[i - 2][0])
        add_across(i)
    add_cores(0)
    assemble(count - 1)
    chunk[-2:] = [carried(i)[0] for i in (count - 2, count - 1)]
    contract(1)
    add_cores(1)
    finish(0)
    results[2] = priors[2] + scale * state[2]
    finish(1)
    return tuple(results)


def any_lines(inputs, omegas, bases, eigens, scale):
    cores = core_total(bases, omegas)
    results = []
    for x, w, b, e, core in zip(inputs, omegas, bases, eigens, cores):
        partial = jnp.dot(x, w, preferred_element_type=jnp.float32)
        share = lax.psum_scatter(partial, "owner", scatter_dimension=0, tiled=True)
        probe = lax.all_gather(share.astype(jnp.bfloat16), "owner", axis=0, tiled=True)
        data = lax.psum_scatter(
            token_contract(x, probe), "context", scatter_dimension=0, tiled=True
        )
        results.append(prior_rows(b, e, core) + scale * data)
    return tuple(results)


def per_device(
    x_attn,
    x_mlp,
    x_down,
    omega_attn,
    omega_mlp,
    omega_down,
    basis_attn,
    basis_mlp,
    basis_down,
    eig_attn,
    eig_mlp,
    eig_down,
):
    inputs = (x_attn, x_mlp, x_down)
    omegas = (omega_attn, omega_mlp, omega_down)
    bases = (basis_attn, basis_mlp, basis_down)
    eigens = (eig_attn, eig_mlp, eig_down)
    scale = 0.1 / (x_attn.shape[0] * lax.axis_size("context"))
    fours = lax.axis_size("owner") == 4 and lax.axis_size("context") == 4
    run = lines_of_four if fours else any_lines
    return run(inputs, omegas, bases, eigens, scale)


def solution(mesh):
    placed = (
        P(("section", "context"), "owner"),
        P(("section", "context"), "owner"),
        P(("section", "context"), "owner"),
        P(("section", "owner"), None),
        P(("section", "owner"), None),
        P(("section", "owner"), None),
        P(("section", "owner"), None),
        P(("section", "owner"), None),
        P(("section", "owner"), None),
        P("section"),
        P("section"),
        P("section"),
    )
    return jax.shard_map(
        per_device,
        mesh=mesh,
        in_specs=placed,
        out_specs=(
            P(("section", "owner", "context"), None),
            P(("section", "owner", "context"), None),
            P(("section", "owner", "context"), None),
        ),
        check_vma=False,
    )
```

```python
import math

import jax
import jax.numpy as jnp
from jax import lax
from jax.experimental import pallas as pl
from jax.experimental.pallas import tpu as pltpu
from jax.sharding import PartitionSpec as P

INWARD = ((0, 1), (3, 2))
ACROSS = ((1, 2), (2, 1))
OUTWARD = ((1, 0), (2, 3))
PAIRED = ((0, 1), (1, 0), (2, 3), (3, 2))
SKIPPED = ((0, 2), (2, 0), (1, 3), (3, 1))
CHUNKS = ((2, 8), (2, 8), (0, 8), (0, 8), (1, 8), (1, 8))
CARRIER = 2
FINE, COARSE = 65535.0, 32500.0
MIB = 1024 * 1024
FIRST = (((0,), (0,)), ((), ()))
ANYWHERE = pl.BlockSpec(memory_space=pl.ANY)


def token_contract(inputs, probe):
    return lax.dot_general(inputs, probe, FIRST, preferred_element_type=jnp.float32)


def prior_rows(basis, eigen, core):
    rows = basis.shape[0] // lax.axis_size("context")
    picked = lax.dynamic_slice_in_dim(basis, lax.axis_index("context") * rows, rows, 0)
    weighted = eigen[:, None] * core
    return 0.9 * jnp.dot(picked.astype(jnp.float32), weighted, precision=lax.Precision.HIGHEST)


def core_total(bases, omegas):
    size = lax.axis_size("context")
    rank = omegas[0].shape[1]
    share = rank // size
    start = lax.axis_index("context") * share
    mine = [
        token_contract(lax.dynamic_slice_in_dim(b, start, share, 1), w)
        for b, w in zip(bases, omegas)
    ]
    summed = lax.psum(jnp.concatenate(mine, 0), "owner")
    whole = lax.all_gather(summed, "context", axis=0)
    whole = whole.reshape(size, len(bases), share, rank)
    return [whole[:, k].reshape(rank, rank) for k in range(len(bases))]


class Order:
    def __init__(self):
        self.last = ()

    def call(self, kernel, operands, out, after=(), vmem=8 * MIB, **rest):
        held = (*self.last, *after)
        count = len(operands)
        outs = out if isinstance(out, tuple) else (out,)
        steps = len(rest.get("grid", ()))

        def body(*refs):
            results = refs[count + len(held) :]
            mark = results[len(outs)]
            mark[...] = jnp.zeros_like(mark)
            kernel(*refs[:count], *results[: len(outs)], *results[len(outs) + 1 :])

        whole = pl.BlockSpec(memory_space=pltpu.VMEM)
        specs = rest.pop("in_specs", [whole] * count)
        out_specs = rest.pop("out_specs", [whole] * len(outs))
        zeros = (0, 0)
        marked = pl.BlockSpec((8, 128), lambda *_: zeros) if steps else whole
        *result, mark = pl.pallas_call(
            body,
            out_shape=(*outs, jax.ShapeDtypeStruct((8, 128), jnp.float32)),
            in_specs=[*specs, *[ANYWHERE] * len(held)],
            out_specs=[*out_specs, marked],
            compiler_params=pltpu.CompilerParams(vmem_limit_bytes=vmem),
            **rest,
        )(*operands, *held)
        self.last = (mark,)
        return tuple(result) if isinstance(out, tuple) else result[0]

    def gate(self, array, after=(), hbm=False):
        return self.call(
            lambda *_: None,
            (array,),
            pltpu.HBM(array.shape, array.dtype) if hbm else jax.ShapeDtypeStruct(array.shape, array.dtype),
            after,
            MIB,
            in_specs=[pl.BlockSpec(memory_space=pltpu.HBM) if hbm else ANYWHERE],
            out_specs=[pl.BlockSpec(memory_space=pltpu.HBM) if hbm else ANYWHERE],
            input_output_aliases={0: 0},
        )


def probe_rows(order, inputs, omega, start, rows, turned):
    tile = math.gcd(512, start, rows)
    rank = omega.shape[1]
    first = start // tile

    def kernel(x, w, out):
        if turned:
            out[...] = token_contract(x[...], w[...])
        else:
            out[...] = jnp.dot(x[...], w[...], preferred_element_type=jnp.float32)

    depth = omega.shape[0]
    if turned:
        spec = pl.BlockSpec((depth, tile), lambda i: (0, first + i))
    else:
        spec = pl.BlockSpec((tile, depth), lambda i: (first + i, 0))
    return order.call(
        kernel,
        (inputs, omega),
        jax.ShapeDtypeStruct((rows, rank), jnp.float32),
        vmem=52 * MIB,
        grid=(rows // tile,),
        in_specs=[spec, pl.BlockSpec((depth, rank), lambda i: (0, 0))],
        out_specs=[pl.BlockSpec((tile, rank), lambda i: (i, 0))],
    )


def third(rows):
    return -(-rows // 24) * 8


def peaks(values):
    return jnp.maximum(jnp.max(jnp.abs(values), axis=1, keepdims=True), 1e-30)


def diagonal(rows, rank):
    shape = (rows, rank)
    return lax.broadcasted_iota(jnp.int32, shape, 0) == lax.broadcasted_iota(jnp.int32, shape, 1)


def pack(value, out, plain):
    group = third(plain)
    left = plain - 2 * group
    rank = value.shape[1]
    peak = peaks(value[:plain, :])
    scale = FINE / peak
    first = jnp.round(value[:group, :] * scale[:group])
    second = jnp.round(value[group : 2 * group, :] * scale[group : 2 * group])
    last = jnp.round(value[2 * group : plain, :] * (COARSE / peak[2 * group :]))
    high = jnp.round(last * (1 / 255))
    low = last - high * 255
    first, second = first * 256, second * 256
    out[:left, :] = first[:left] + high
    out[group : group + left, :] = second[:left] + low
    if left < group:
        out[left:group, :] = first[left:]
        out[group + left : 2 * group, :] = second[left:]
    out[2 * group : 2 * group + 8, :] = jnp.zeros((8, rank), jnp.float32)
    for k, start in enumerate(range(0, plain, rank)):
        part = peak[start : start + rank]
        row = jnp.where(diagonal(part.shape[0], rank), part, 0.0)
        out[2 * group + k : 2 * group + k + 1, :] = jnp.sum(row, axis=0, keepdims=True)
    if value.shape[0] > plain:
        out[2 * group + 8 :, :] = value[plain:, :]


def add_packed(mine, packed, plain):
    group = third(plain)
    left = plain - 2 * group
    rank = mine.shape[1]
    pieces = []
    for k, start in enumerate(range(0, plain, rank)):
        mask = diagonal(min(rank, plain - start), rank)
        row = jnp.where(mask, packed[2 * group + k : 2 * group + k + 1, :], 0.0)
        pieces.append(jnp.sum(row, axis=1, keepdims=True))
    peak = jnp.concatenate(pieces, 0)
    unit = peak * (1 / FINE)
    first, second = packed[:group, :], packed[group : 2 * group, :]
    whole = jnp.round(first * (1 / 256))
    high = first - whole * 256
    other = jnp.round(second * (1 / 256))
    low = second - other * 256
    last = high[:left] * 255 + low[:left]
    return (
        (0, group, mine[:group, :] + whole * unit[:group]),
        (group, 2 * group, mine[group : 2 * group, :] + other * unit[group : 2 * group]),
        (2 * group, plain, mine[2 * group : plain, :] + last * (peak[2 * group :] * (1 / COARSE))),
    )


def packed_shape(value, plain):
    rows = 2 * third(plain) + 8 + value.shape[0] - plain
    return jax.ShapeDtypeStruct((rows, value.shape[1]), jnp.float32)


def packed(order, partial, plain):
    return order.call(
        lambda value, out: pack(value, out, plain), (partial,), packed_shape(partial, plain)
    )


def paired(order, partial, arrived, plain):
    def kernel(mine, theirs, out, message):
        for start, stop, rows in add_packed(mine, theirs, plain):
            out[start:stop, :] = rows
        if mine.shape[0] > plain:
            out[plain:, :] = mine[plain:, :] + theirs[2 * third(plain) + 8 :, :]
        pack(out, message, plain)

    shape = jax.ShapeDtypeStruct(partial.shape, jnp.float32)
    return order.call(kernel, (partial, arrived), (shape, packed_shape(partial, plain)))


def rounded(order, pair, arrived, plain):
    rows, rank = pair.shape
    exact = rows - plain

    def kernel(mine, theirs, out):
        for start, stop, total in add_packed(mine, theirs, plain):
            out[start:stop, :] = total.astype(jnp.bfloat16)
        if exact:
            rest = mine[plain:, :] + theirs[2 * third(plain) + 8 :, :]
            for i in range(3):
                term = rest.astype(jnp.bfloat16)
                out[plain + i * exact : plain + (i + 1) * exact, :] = term
                rest = rest - term.astype(jnp.float32)

    shape = jax.ShapeDtypeStruct((plain + 3 * exact, rank), jnp.bfloat16)
    return order.call(kernel, (pair, arrived), shape)


def data_rows(order, inputs, probe, piece, pieces, data):
    features = inputs.shape[0]
    tokens, rank = probe.shape
    tile = -(-features // 64) * 16
    tiles = pl.cdiv(features, tile) // pieces
    first = piece * tiles

    def kernel(x, p, *refs):
        refs[-1][...] = jnp.dot(x[...], p[...], preferred_element_type=jnp.float32)

    before = () if data is None else (data,)
    return order.call(
        kernel,
        (inputs, probe, *before),
        pltpu.HBM((features, rank), jnp.float32),
        vmem=52 * MIB,
        grid=(tiles,),
        in_specs=[
            pl.BlockSpec((tile, tokens), lambda i: (first + i, 0)),
            pl.BlockSpec((tokens, rank), lambda i: (0, 0)),
            *[ANYWHERE] * len(before),
        ],
        out_specs=[pl.BlockSpec((tile, rank), lambda i: (first + i, 0))],
        input_output_aliases={2: 0} if before else {},
    )


def data_parts(order, inputs, probe, after):
    tokens, rank = probe.shape
    quarter = inputs.shape[1] // 4
    shape = jax.ShapeDtypeStruct((2, quarter, rank), jnp.float32)
    out_spec = pl.BlockSpec((1, quarter, rank), lambda i: (i, 0, 0))

    def kernel(x, p, given, kept):
        odd = lax.axis_index("context") % 2 == 1
        product = token_contract(x[...], p[...])
        given[0] = jnp.where(odd, product[:quarter], product[quarter:])
        kept[0] = jnp.where(odd, product[quarter:], product[:quarter])

    return order.call(
        kernel,
        (inputs, probe),
        (shape, shape),
        after,
        vmem=52 * MIB,
        grid=(2,),
        in_specs=[
            pl.BlockSpec((tokens, 2 * quarter), lambda i: (0, i)),
            pl.BlockSpec((tokens, rank), lambda i: (0, 0)),
        ],
        out_specs=[out_spec, out_spec],
    )


def core_summed(order, kept, arrived):
    rows, rank = kept.shape[1:]

    def kernel(mine, theirs, stays, message, given):
        high = lax.select(lax.axis_index("context") >= 2, 1, 0)
        given[...] = mine[1 - high] + theirs[1 - high]
        stays[...] = mine[high] + theirs[high]
        pack(given, message, rows)

    shape = jax.ShapeDtypeStruct((rows, rank), jnp.float32)
    return order.call(
        kernel,
        (kept, arrived),
        (shape, packed_shape(shape, rows)),
        scratch_shapes=[pltpu.VMEM((rows, rank), jnp.float32)],
        vmem=12 * MIB,
    )


def finished(order, basis, eigen, cores, place, shares, scale):
    rows, rank = basis.shape
    part = cores.shape[0] // 4
    share = rank // 4

    def kernel(b, e, c, *refs):
        out = refs[-1]
        core = jnp.concatenate(
            [c[i * part + place * share : i * part + (place + 1) * share, :] for i in range(4)], 0
        )
        column = jnp.sum(jnp.where(diagonal(rank, rank), e[...], 0.0), axis=1, keepdims=True)
        rest = column * core
        prior = jnp.zeros((rows, rank), jnp.float32)
        for _ in range(3):
            term = rest.astype(jnp.bfloat16)
            prior += jnp.dot(b[...], term, preferred_element_type=jnp.float32)
            rest = rest - term.astype(jnp.float32)
        if len(refs) == 2:
            out[...] = 0.9 * prior + scale * refs[0][...]
        else:
            for start, stop, total in add_packed(refs[0], refs[1], rows):
                out[start:stop, :] = 0.9 * prior[start:stop] + scale * total

    shape = jax.ShapeDtypeStruct((rows, rank), jnp.float32)
    operands = (basis, eigen.reshape(1, rank), cores, *shares)
    return order.call(kernel, operands, shape, vmem=16 * MIB)


def core_parts(order, bases, omegas, after):
    rank = omegas[0].shape[1]
    share = rank // lax.axis_size("context")
    count = len(bases)

    def kernel(*refs):
        out, product = refs[-2:]
        start = pl.multiple_of(lax.axis_index("context") * share, share)
        for k in range(count):
            product[...] = token_contract(refs[k][...], refs[count + k][...])
            out[k * share : (k + 1) * share, :] = product[pl.ds(start, share), :]

    shape = jax.ShapeDtypeStruct((count * share, rank), jnp.float32)
    scratch = [pltpu.VMEM((rank, rank), jnp.float32)]
    return order.call(kernel, (*bases, *omegas), shape, after, 52 * MIB, scratch_shapes=scratch)


def lines_of_four(inputs, omegas, bases, eigens, scale):
    place = lax.axis_index("owner")
    inner = (place == 1) | (place == 2)
    turned = [x.shape[1] % 128 != 0 for x in inputs]
    inputs = [x.T if t else x for x, t in zip(inputs, turned)]
    order = Order()
    jobs = [k for k, _ in CHUNKS]
    count = len(jobs)
    partial, plain, message, inward, pair, across, probe, outward, chunk = (
        [None] * count for _ in range(9)
    )
    state = [None] * 3
    results = [None] * 3
    rank = omegas[0].shape[1]

    def multiply(i):
        k, share = CHUNKS[i]
        unit = inputs[k].shape[1 if turned[k] else 0] // 16
        start = unit * sum(n for j, n in CHUNKS[:i] if j == k)
        rows = unit * share
        partial[i] = probe_rows(order, inputs[k], omegas[k], start, rows, turned[k])
        if i == CARRIER:
            partial[i] = jnp.concatenate([partial[i], cores], 0)
        plain[i] = rows
        message[i] = packed(order, partial[i], rows)

    def send(i, after=()):
        if after:
            message[i] = order.gate(message[i], after)
        inward[i] = lax.ppermute(message[i], "owner", INWARD)

    def add_pair(i):
        pair[i], sums = paired(order, partial[i], inward[i], plain[i])
        across[i] = lax.ppermute(sums, "owner", ACROSS)

    def add_across(i):
        probe[i] = rounded(order, pair[i], across[i], plain[i])
        outward[i] = lax.ppermute(probe[i], "owner", OUTWARD)

    def carried(i):
        whole = lax.select(inner, probe[i], outward[i])
        if i != CARRIER:
            return whole, None
        terms = whole[plain[i] :].reshape(3, cores.shape[0], rank).astype(jnp.float32)
        return whole[: plain[i]], terms[0] + (terms[1] + terms[2])

    def probes(k):
        return jnp.concatenate([chunk[i] for i in range(count) if jobs[i] == k], 0)

    def contract(k, after=()):
        given, kept = data_parts(order, inputs[k], probes(k), after)
        state[k] = kept, given

    def share_out(k, now=False):
        if turned[k]:
            data = order.gate(state[k], (), True)
            state[k] = (lax.psum_scatter(data, "context", scatter_dimension=0, tiled=True),)
        else:
            kept, given = state[k]
            given = given if now else order.gate(given)
            state[k] = kept, lax.ppermute(given, "context", PAIRED)

    def add_cores(k):
        stays, given = core_summed(order, *state[k])
        state[k] = stays, lax.ppermute(given, "context", SKIPPED)

    def finish(k):
        results[k] = finished(order, picked[k], eigens[k], whole, k, state[k], scale)

    def receive(i):
        chunk[i], total = carried(i)
        return total

    def swapped(array, pairs, upper):
        theirs = lax.ppermute(order.gate(array), "context", pairs)
        return jnp.concatenate(
            [lax.select(upper, theirs, array), lax.select(upper, array, theirs)], 0
        )

    context = lax.axis_index("context")
    quarters = [b.shape[0] // 4 for b in bases]
    picked = [lax.dynamic_slice_in_dim(b, context * n, n, 0) for b, n in zip(bases, quarters)]
    multiply(0)
    send(0)
    multiply(1)
    for i in range(count):
        ahead = i + 1 < count
        shrinks = ahead and message[i].shape[0] > message[i + 1].shape[0]
        came = (inward[i],) if i < 2 else (inward[i], outward[i - 2])
        if shrinks:
            add_pair(i)
        if ahead:
            send(i + 1, came)
        if not shrinks:
            add_pair(i)
        if i > 0:
            add_across(i - 1)
        if i == 4:
            share_out(2)
            pairs = swapped(totals, PAIRED, context % 2 == 1)
        if i == 5:
            whole = swapped(pairs, SKIPPED, context >= 2)
        if i == CARRIER - 2:
            cores = core_parts(order, bases, omegas, picked)
        if i + 2 < count:
            multiply(i + 2)
        if i > 0:
            got = receive(i - 1)
            totals = got if i - 1 == CARRIER else totals if i > CARRIER + 1 else None
        if i in (2, 3):
            state[2] = data_rows(order, inputs[2], probes(2), i - 2, 2, state[2])
        if i == 4:
            contract(0)
    add_across(count - 1)
    share_out(0)
    add_cores(0)
    receive(count - 1)
    contract(1)
    share_out(1, True)
    add_cores(1)
    finish(2)
    finish(0)
    finish(1)
    return tuple(results)


def any_lines(inputs, omegas, bases, eigens, scale):
    cores = core_total(bases, omegas)
    results = []
    for x, w, b, e, core in zip(inputs, omegas, bases, eigens, cores):
        partial = jnp.dot(x, w, preferred_element_type=jnp.float32)
        share = lax.psum_scatter(partial, "owner", scatter_dimension=0, tiled=True)
        probe = lax.all_gather(share.astype(jnp.bfloat16), "owner", axis=0, tiled=True)
        data = lax.psum_scatter(
            token_contract(x, probe), "context", scatter_dimension=0, tiled=True
        )
        results.append(prior_rows(b, e, core) + scale * data)
    return tuple(results)


def per_device(
    x_attn,
    x_mlp,
    x_down,
    omega_attn,
    omega_mlp,
    omega_down,
    basis_attn,
    basis_mlp,
    basis_down,
    eig_attn,
    eig_mlp,
    eig_down,
):
    inputs = (x_attn, x_mlp, x_down)
    omegas = (omega_attn, omega_mlp, omega_down)
    bases = (basis_attn, basis_mlp, basis_down)
    eigens = (eig_attn, eig_mlp, eig_down)
    scale = 0.1 / (x_attn.shape[0] * lax.axis_size("context"))
    fours = lax.axis_size("owner") == 4 and lax.axis_size("context") == 4
    run = lines_of_four if fours else any_lines
    return run(inputs, omegas, bases, eigens, scale)


def solution(mesh):
    placed = (
        P(("section", "context"), "owner"),
        P(("section", "context"), "owner"),
        P(("section", "context"), "owner"),
        P(("section", "owner"), None),
        P(("section", "owner"), None),
        P(("section", "owner"), None),
        P(("section", "owner"), None),
        P(("section", "owner"), None),
        P(("section", "owner"), None),
        P("section"),
        P("section"),
        P("section"),
    )
    return jax.shard_map(
        per_device,
        mesh=mesh,
        in_specs=placed,
        out_specs=(
            P(("section", "owner", "context"), None),
            P(("section", "owner", "context"), None),
            P(("section", "owner", "context"), None),
        ),
        check_vma=False,
    )
```

```python
import math

import jax
import jax.numpy as jnp
from jax import lax
from jax.experimental import pallas as pl
from jax.experimental.pallas import tpu as pltpu
from jax.sharding import PartitionSpec as P

INWARD = ((0, 1), (3, 2))
ACROSS = ((1, 2), (2, 1))
OUTWARD = ((1, 0), (2, 3))
PAIRED = ((0, 1), (1, 0), (2, 3), (3, 2))
SKIPPED = ((0, 2), (2, 0), (1, 3), (3, 1))
CHUNKS = ((2, 8), (2, 8), (0, 8), (0, 8), (1, 8), (1, 8))
CARRIER = 2
TERMS = 3
STEPS = ("GB", "GBR", "BGR", "GBR", "GBR", "BR")
SWAPS, SHARED, ATTN, PIECES = (4, 4), 4, 4, (2, 3)
WAITS = 1
SELECTED = True
FENCED = False
ROOM = 52
SPLIT = 2
SUMMED = 5
EARLY = 2
FINE, COARSE = 65535.0, 32500.0
MIB = 1024 * 1024
FIRST = (((0,), (0,)), ((), ()))
ANYWHERE = pl.BlockSpec(memory_space=pl.ANY)


def token_contract(inputs, probe):
    return lax.dot_general(inputs, probe, FIRST, preferred_element_type=jnp.float32)


def prior_rows(basis, eigen, core):
    rows = basis.shape[0] // lax.axis_size("context")
    picked = lax.dynamic_slice_in_dim(basis, lax.axis_index("context") * rows, rows, 0)
    weighted = eigen[:, None] * core
    return 0.9 * jnp.dot(picked.astype(jnp.float32), weighted, precision=lax.Precision.HIGHEST)


def core_total(bases, omegas):
    size = lax.axis_size("context")
    rank = omegas[0].shape[1]
    share = rank // size
    start = lax.axis_index("context") * share
    mine = [
        token_contract(lax.dynamic_slice_in_dim(b, start, share, 1), w)
        for b, w in zip(bases, omegas)
    ]
    summed = lax.psum(jnp.concatenate(mine, 0), "owner")
    whole = lax.all_gather(summed, "context", axis=0)
    whole = whole.reshape(size, len(bases), share, rank)
    return [whole[:, k].reshape(rank, rank) for k in range(len(bases))]


class Order:
    def __init__(self):
        self.last = ()

    def call(self, kernel, operands, out, after=(), vmem=8 * MIB, **rest):
        held = (*self.last, *after)
        count = len(operands)
        outs = out if isinstance(out, tuple) else (out,)
        steps = len(rest.get("grid", ()))

        def body(*refs):
            results = refs[count + len(held) :]
            mark = results[len(outs)]
            mark[...] = jnp.zeros_like(mark)
            kernel(*refs[:count], *results[: len(outs)], *results[len(outs) + 1 :])

        whole = pl.BlockSpec(memory_space=pltpu.VMEM)
        specs = rest.pop("in_specs", [whole] * count)
        out_specs = rest.pop("out_specs", [whole] * len(outs))
        zeros = (0, 0)
        marked = pl.BlockSpec((8, 128), lambda *_: zeros) if steps else whole
        *result, mark = pl.pallas_call(
            body,
            out_shape=(*outs, jax.ShapeDtypeStruct((8, 128), jnp.float32)),
            in_specs=[*specs, *[ANYWHERE] * len(held)],
            out_specs=[*out_specs, marked],
            cost_estimate=pl.CostEstimate(flops=10**9, bytes_accessed=10**7, transcendentals=0),
            compiler_params=pltpu.CompilerParams(vmem_limit_bytes=vmem),
            **rest,
        )(*operands, *held)
        self.last = (mark,)
        return tuple(result) if isinstance(out, tuple) else result[0]

    def gate(self, array, after=(), hbm=False):
        return self.call(
            lambda *_: None,
            (array,),
            pltpu.HBM(array.shape, array.dtype) if hbm else jax.ShapeDtypeStruct(array.shape, array.dtype),
            after,
            MIB,
            in_specs=[pl.BlockSpec(memory_space=pltpu.HBM) if hbm else ANYWHERE],
            out_specs=[pl.BlockSpec(memory_space=pltpu.HBM) if hbm else ANYWHERE],
            input_output_aliases={0: 0},
        )


def probe_rows(order, inputs, omega, start, rows, turned):
    depth, rank = omega.shape
    shape = jax.ShapeDtypeStruct((rows, rank), jnp.float32)
    tile = math.gcd(512, start, rows)
    first = start // tile

    def kernel(x, w, out):
        if turned:
            out[...] = token_contract(x[...], w[...])
        else:
            out[...] = jnp.dot(x[...], w[...], preferred_element_type=jnp.float32)

    if turned:
        spec = pl.BlockSpec((depth, tile), lambda i: (0, first + i))
    else:
        spec = pl.BlockSpec((tile, depth), lambda i: (first + i, 0))
    return order.call(
        kernel,
        (inputs, omega),
        shape,
        vmem=ROOM * MIB,
        grid=(rows // tile,),
        in_specs=[spec, pl.BlockSpec((depth, rank), lambda i: (0, 0))],
        out_specs=[pl.BlockSpec((tile, rank), lambda i: (i, 0))],
    )


def third(rows):
    return -(-rows // 24) * 8


def peaks(values):
    return jnp.maximum(jnp.max(jnp.abs(values), axis=1, keepdims=True), 1e-30)


def diagonal(rows, rank):
    shape = (rows, rank)
    return lax.broadcasted_iota(jnp.int32, shape, 0) == lax.broadcasted_iota(jnp.int32, shape, 1)


def pack(value, out, plain):
    group = third(plain)
    left = plain - 2 * group
    rank = value.shape[1]
    peak = peaks(value[:plain, :])
    scale = FINE / peak
    first = jnp.round(value[:group, :] * scale[:group])
    second = jnp.round(value[group : 2 * group, :] * scale[group : 2 * group])
    last = jnp.round(value[2 * group : plain, :] * (COARSE / peak[2 * group :]))
    high = jnp.round(last * (1 / 255))
    low = last - high * 255
    first, second = first * 256, second * 256
    out[:left, :] = first[:left] + high
    out[group : group + left, :] = second[:left] + low
    if left < group:
        out[left:group, :] = first[left:]
        out[group + left : 2 * group, :] = second[left:]
    out[2 * group : 2 * group + 8, :] = jnp.zeros((8, rank), jnp.float32)
    for k, start in enumerate(range(0, plain, rank)):
        part = peak[start : start + rank]
        row = jnp.where(diagonal(part.shape[0], rank), part, 0.0)
        out[2 * group + k : 2 * group + k + 1, :] = jnp.sum(row, axis=0, keepdims=True)
    if value.shape[0] > plain:
        out[2 * group + 8 :, :] = value[plain:, :]


def add_packed(mine, packed, plain):
    group = third(plain)
    left = plain - 2 * group
    rank = mine.shape[1]
    pieces = []
    for k, start in enumerate(range(0, plain, rank)):
        mask = diagonal(min(rank, plain - start), rank)
        row = jnp.where(mask, packed[2 * group + k : 2 * group + k + 1, :], 0.0)
        pieces.append(jnp.sum(row, axis=1, keepdims=True))
    peak = jnp.concatenate(pieces, 0)
    unit = peak * (1 / FINE)
    first, second = packed[:group, :], packed[group : 2 * group, :]
    whole = jnp.round(first * (1 / 256))
    high = first - whole * 256
    other = jnp.round(second * (1 / 256))
    low = second - other * 256
    last = high[:left] * 255 + low[:left]
    return (
        (0, group, mine[:group, :] + whole * unit[:group]),
        (group, 2 * group, mine[group : 2 * group, :] + other * unit[group : 2 * group]),
        (2 * group, plain, mine[2 * group : plain, :] + last * (peak[2 * group :] * (1 / COARSE))),
    )


def packed_shape(value, plain):
    rows = 2 * third(plain) + 8 + value.shape[0] - plain
    return jax.ShapeDtypeStruct((rows, value.shape[1]), jnp.float32)


def packed(order, partial, plain, after):
    shape = packed_shape(partial, plain)
    return order.call(lambda value, out: pack(value, out, plain), (partial,), shape, after)


def paired(order, partial, arrived, plain):
    def kernel(mine, theirs, out, message):
        for start, stop, rows in add_packed(mine, theirs, plain):
            out[start:stop, :] = rows
        if mine.shape[0] > plain:
            out[plain:, :] = mine[plain:, :] + theirs[2 * third(plain) + 8 :, :]
        pack(out, message, plain)

    shape = jax.ShapeDtypeStruct(partial.shape, jnp.float32)
    return order.call(kernel, (partial, arrived), (shape, packed_shape(partial, plain)))


def rounded(order, pair, arrived, plain, after):
    rows, rank = pair.shape
    exact = rows - plain

    def kernel(mine, theirs, out):
        for start, stop, total in add_packed(mine, theirs, plain):
            out[start:stop, :] = total.astype(jnp.bfloat16)
        if exact:
            rest = mine[plain:, :] + theirs[2 * third(plain) + 8 :, :]
            for i in range(TERMS):
                term = rest.astype(jnp.bfloat16)
                out[plain + i * exact : plain + (i + 1) * exact, :] = term
                rest = rest - term.astype(jnp.float32)

    shape = jax.ShapeDtypeStruct((plain + TERMS * exact, rank), jnp.bfloat16)
    return order.call(kernel, (pair, arrived), shape, after)


def pieces_of(chunks):
    if not isinstance(chunks, list):
        return [chunks], None
    parts = [array for own, received, _ in chunks for array in (own, received)]

    def fill(refs, probe):
        place = lax.axis_index("owner")
        inner = (place == 1) | (place == 2)
        start = 0
        for i, (_, _, rows) in enumerate(chunks):
            own, received = refs[2 * i], refs[2 * i + 1]
            probe[start : start + rows, :] = jnp.where(inner, own[:rows, :], received[:rows, :])
            start += rows

    return parts, fill


def data_half(order, inputs, chunks, half, before):
    features, tokens = inputs.shape
    parts, fill = pieces_of(chunks)
    rank = parts[0].shape[1]
    quarter = features // 4
    depth = tokens // SPLIT
    shape = pltpu.HBM((2, quarter, rank), jnp.float32)
    out_spec = pl.BlockSpec((1, quarter, rank), lambda i: (half, 0, 0))

    def kernel(x, p, *refs):
        given, kept, total = refs[-3:]
        odd = lax.axis_index("context") % 2 == 1
        step = pl.program_id(0)
        product = jnp.dot(x[...], p[...], preferred_element_type=jnp.float32)

        @pl.when(step == 0)
        def _():
            total[...] = product

        @pl.when(step > 0)
        def _():
            total[...] += product

        @pl.when((step == SPLIT - 1) & odd)
        def _():
            given[0] = total[:quarter, :]
            kept[0] = total[quarter:, :]

        @pl.when((step == SPLIT - 1) & jnp.logical_not(odd))
        def _():
            kept[0] = total[:quarter, :]
            given[0] = total[quarter:, :]

    return order.call(
        kernel,
        (inputs, *parts, *before),
        (shape, shape),
        vmem=ROOM * MIB,
        grid=(SPLIT,),
        in_specs=[
            pl.BlockSpec((2 * quarter, depth), lambda i: (half, i)),
            pl.BlockSpec((depth, rank), lambda i: (i, 0)),
            *[ANYWHERE] * len(before),
        ],
        out_specs=[out_spec, out_spec],
        scratch_shapes=[pltpu.VMEM((2 * quarter, rank), jnp.float32)],
        input_output_aliases={2: 0, 3: 1} if before else {},
    )


def data_parts(order, inputs, chunks, after):
    tokens = inputs.shape[0]
    parts, fill = pieces_of(chunks)
    rank = parts[0].shape[1]
    quarter = inputs.shape[1] // 4
    shape = jax.ShapeDtypeStruct((2, quarter, rank), jnp.float32)
    out_spec = pl.BlockSpec((1, quarter, rank), lambda i: (i, 0, 0))

    def kernel(x, *refs):
        given, kept, probe = refs[-3:] if fill else (*refs[-2:], refs[0])
        if fill:
            pl.when(pl.program_id(0) == 0)(lambda: fill(refs, probe))
        odd = lax.axis_index("context") % 2 == 1
        product = token_contract(x[...], probe[...])
        given[0] = jnp.where(odd, product[:quarter], product[quarter:])
        kept[0] = jnp.where(odd, product[quarter:], product[:quarter])

    return order.call(
        kernel,
        (inputs, *parts),
        (shape, shape),
        after,
        vmem=ROOM * MIB,
        grid=(2,),
        in_specs=[
            pl.BlockSpec((tokens, 2 * quarter), lambda i: (0, i)),
            *[pl.BlockSpec(p.shape, lambda i: (0, 0)) for p in parts],
        ],
        out_specs=[out_spec, out_spec],
        scratch_shapes=[pltpu.VMEM((tokens, rank), jnp.bfloat16)] if fill else [],
    )


def core_summed(order, kept, arrived):
    rows, rank = kept.shape[1:]

    def kernel(mine, theirs, stays, message, given):
        high = lax.select(lax.axis_index("context") >= 2, 1, 0)
        given[...] = mine[1 - high] + theirs[1 - high]
        stays[...] = mine[high] + theirs[high]
        pack(given, message, rows)

    shape = jax.ShapeDtypeStruct((rows, rank), jnp.float32)
    return order.call(
        kernel,
        (kept, arrived),
        (shape, packed_shape(shape, rows)),
        scratch_shapes=[pltpu.VMEM((rows, rank), jnp.float32)],
        vmem=(8 + rows // 96) * MIB,
    )


def finished(order, basis, eigen, cores, place, shares, scale):
    rows, rank = basis.shape
    part = cores.shape[0] // 4
    share = rank // 4

    def kernel(b, e, c, *refs):
        out = refs[-1]
        core = jnp.concatenate(
            [c[i * part + place * share : i * part + (place + 1) * share, :] for i in range(4)], 0
        )
        column = jnp.sum(jnp.where(diagonal(rank, rank), e[...], 0.0), axis=1, keepdims=True)
        rest = column * core
        prior = jnp.zeros((rows, rank), jnp.float32)
        for _ in range(3):
            term = rest.astype(jnp.bfloat16)
            prior += jnp.dot(b[...], term, preferred_element_type=jnp.float32)
            rest = rest - term.astype(jnp.float32)
        if len(refs) == 2:
            out[...] = 0.9 * prior + scale * refs[0][...]
        else:
            for start, stop, total in add_packed(refs[0], refs[1], rows):
                out[start:stop, :] = 0.9 * prior[start:stop] + scale * total

    shape = jax.ShapeDtypeStruct((rows, rank), jnp.float32)
    operands = (basis, eigen.reshape(1, rank), cores, *shares)
    return order.call(kernel, operands, shape, vmem=24 * MIB)


def core_parts(order, bases, omegas):
    rank = omegas[0].shape[1]
    share = rank // lax.axis_size("context")
    count = len(bases)

    def kernel(*refs):
        out, product = refs[-2:]
        start = pl.multiple_of(lax.axis_index("context") * share, share)
        for k in range(count):
            product[...] = token_contract(refs[k][...], refs[count + k][...])
            out[k * share : (k + 1) * share, :] = product[pl.ds(start, share), :]

    shape = jax.ShapeDtypeStruct((count * share, rank), jnp.float32)
    scratch = [pltpu.VMEM((rank, rank), jnp.float32)]
    return order.call(kernel, (*bases, *omegas), shape, vmem=ROOM * MIB, scratch_shapes=scratch)


def lines_of_four(inputs, omegas, bases, eigens, scale):
    turned = [x.shape[1] % 128 != 0 for x in inputs]
    inputs = [
        pltpu.with_memory_space_constraint(x.T if t else x, pltpu.HBM) if FENCED else x.T if t else x
        for x, t in zip(inputs, turned)
    ]
    order = Order()
    jobs = [k for k, _ in CHUNKS]
    count = len(jobs)
    partial, plain, message, inward, pair, across, probe, outward = (
        [None] * count for _ in range(8)
    )
    state = [None] * 3
    results = [None] * 3
    rank = omegas[0].shape[1]

    def multiply(i, after=()):
        k, share = CHUNKS[i]
        unit = inputs[k].shape[1 if turned[k] else 0] // 16
        start = unit * sum(n for j, n in CHUNKS[:i] if j == k)
        rows = unit * share
        partial[i] = probe_rows(order, inputs[k], omegas[k], start, rows, turned[k])
        if i == CARRIER:
            partial[i] = jnp.concatenate([partial[i], cores], 0)
        plain[i] = rows
        message[i] = packed(order, partial[i], rows, after)

    def send(i, after=()):
        if after:
            message[i] = order.gate(message[i], after)
        inward[i] = lax.ppermute(message[i], "owner", INWARD)

    def add_pair(i):
        pair[i], sums = paired(order, partial[i], inward[i], plain[i])
        across[i] = lax.ppermute(sums, "owner", ACROSS)

    def add_across(i, after=()):
        probe[i] = rounded(order, pair[i], across[i], plain[i], after)
        outward[i] = lax.ppermute(probe[i], "owner", OUTWARD)

    def carried(i):
        place = lax.axis_index("owner")
        inner = (place == 1) | (place == 2)
        terms = lax.select(inner, probe[i][plain[i] :], outward[i][plain[i] :])
        return jnp.sum(terms.reshape(TERMS, cores.shape[0], rank).astype(jnp.float32), 0)

    def probes(k):
        mine = [i for i in range(count) if jobs[i] == k]
        if not SELECTED:
            return [(probe[i], outward[i], plain[i]) for i in mine]
        place = lax.axis_index("owner")
        inner = (place == 1) | (place == 2)
        whole = [lax.select(inner, probe[i], outward[i])[: plain[i]] for i in mine]
        return jnp.concatenate(whole, 0)

    def contract(k, after=()):
        given, kept = data_parts(order, inputs[k], probes(k), after)
        state[k] = kept, given

    def share_out(k, now=False):
        kept, given = state[k]
        given = given if now else order.gate(given, (), turned[k])
        state[k] = kept, lax.ppermute(given, "context", PAIRED)

    def add_cores(k):
        stays, given = core_summed(order, *state[k])
        state[k] = stays, lax.ppermute(given, "context", SKIPPED)

    def finish(k):
        results[k] = finished(order, picked[k], eigens[k], whole, k, state[k], scale)

    def swapped(array, pairs, upper):
        theirs = lax.ppermute(order.gate(array), "context", pairs)
        return jnp.concatenate(
            [lax.select(upper, theirs, array), lax.select(upper, array, theirs)], 0
        )

    context = lax.axis_index("context")
    quarters = [b.shape[0] // 4 for b in bases]
    picked = [lax.dynamic_slice_in_dim(b, context * n, n, 0) for b, n in zip(bases, quarters)]
    halves = ()
    multiply(0)
    send(0)
    multiply(1)
    for i in range(count):
        for act in STEPS[i]:
            if act == "B":
                add_pair(i)
            elif act == "R":
                add_across(i - 1)
            else:
                send(i + 1, (inward[i],) if i < 2 else (inward[i], outward[i - 2]))
        if i == SWAPS[0]:
            pairs = swapped(totals, PAIRED, context % 2 == 1)
        if i == SWAPS[1]:
            whole = swapped(pairs, SKIPPED, context >= 2)
        if i == SHARED:
            share_out(2)
        if i == CARRIER - 2:
            cores = core_parts(order, bases, omegas)
        if i + 2 < count:
            multiply(i + 2, picked if i == 0 else ())
        if i in PIECES:
            halves = data_half(order, inputs[2], probes(2), PIECES.index(i), halves)
            state[2] = halves[1], halves[0]
        if i == ATTN:
            contract(0, (whole,) if WAITS == 2 else ())
        if i == CARRIER + 1:
            totals = carried(CARRIER)
        if i == 5:
            share_out(0)
        if i == SUMMED:
            add_cores(2)
        if i == 5:
            add_cores(0)
    add_across(count - 1)
    if EARLY == 1:
        finish(2)
    contract(1, (whole,) if WAITS == 1 else ())
    share_out(1, True)
    if EARLY == 2:
        finish(2)
    add_cores(1)
    if EARLY == 0:
        finish(2)
    finish(0)
    finish(1)
    return tuple(results)


def any_lines(inputs, omegas, bases, eigens, scale):
    cores = core_total(bases, omegas)
    results = []
    for x, w, b, e, core in zip(inputs, omegas, bases, eigens, cores):
        partial = jnp.dot(x, w, preferred_element_type=jnp.float32)
        share = lax.psum_scatter(partial, "owner", scatter_dimension=0, tiled=True)
        probe = lax.all_gather(share.astype(jnp.bfloat16), "owner", axis=0, tiled=True)
        data = lax.psum_scatter(
            token_contract(x, probe), "context", scatter_dimension=0, tiled=True
        )
        results.append(prior_rows(b, e, core) + scale * data)
    return tuple(results)


def per_device(
    x_attn,
    x_mlp,
    x_down,
    omega_attn,
    omega_mlp,
    omega_down,
    basis_attn,
    basis_mlp,
    basis_down,
    eig_attn,
    eig_mlp,
    eig_down,
):
    inputs = (x_attn, x_mlp, x_down)
    omegas = (omega_attn, omega_mlp, omega_down)
    bases = (basis_attn, basis_mlp, basis_down)
    eigens = (eig_attn, eig_mlp, eig_down)
    scale = 0.1 / (x_attn.shape[0] * lax.axis_size("context"))
    fours = lax.axis_size("owner") == 4 and lax.axis_size("context") == 4
    run = lines_of_four if fours else any_lines
    return run(inputs, omegas, bases, eigens, scale)


def solution(mesh):
    placed = (
        P(("section", "context"), "owner"),
        P(("section", "context"), "owner"),
        P(("section", "context"), "owner"),
        P(("section", "owner"), None),
        P(("section", "owner"), None),
        P(("section", "owner"), None),
        P(("section", "owner"), None),
        P(("section", "owner"), None),
        P(("section", "owner"), None),
        P("section"),
        P("section"),
        P("section"),
    )
    return jax.shard_map(
        per_device,
        mesh=mesh,
        in_specs=placed,
        out_specs=(
            P(("section", "owner", "context"), None),
            P(("section", "owner", "context"), None),
            P(("section", "owner", "context"), None),
        ),
        check_vma=False,
    )
```

```python
import math

import jax
import jax.numpy as jnp
from jax import lax
from jax.experimental import pallas as pl
from jax.experimental.pallas import tpu as pltpu
from jax.sharding import PartitionSpec as P

INWARD = ((0, 1), (3, 2))
ACROSS = ((1, 2), (2, 1))
OUTWARD = ((1, 0), (2, 3))
PAIRED = ((0, 1), (1, 0), (2, 3), (3, 2))
SKIPPED = ((0, 2), (2, 0), (1, 3), (3, 1))
CHUNKS = ((2, 8), (2, 8), (0, 8), (0, 8), (1, 8), (1, 8))
CARRIER = 2
TERMS = 2
STEPS = ("GB", "GBR", "BGR", "GBR", "GBR", "BR")
SWAPS, SHARED, ATTN, PIECES = (4, 4), 4, 4, (2, 3)
WAITS = 1
SELECTED = True
FENCED = False
ROOM = 52
SPLIT = 2
SUMMED = 5
EARLY = 2
FINE, COARSE = 65535.0, 32500.0
MIB = 1024 * 1024
FIRST = (((0,), (0,)), ((), ()))
ANYWHERE = pl.BlockSpec(memory_space=pl.ANY)


def token_contract(inputs, probe):
    return lax.dot_general(inputs, probe, FIRST, preferred_element_type=jnp.float32)


def prior_rows(basis, eigen, core):
    rows = basis.shape[0] // lax.axis_size("context")
    picked = lax.dynamic_slice_in_dim(basis, lax.axis_index("context") * rows, rows, 0)
    weighted = eigen[:, None] * core
    return 0.9 * jnp.dot(picked.astype(jnp.float32), weighted, precision=lax.Precision.HIGHEST)


def core_total(bases, omegas):
    size = lax.axis_size("context")
    rank = omegas[0].shape[1]
    share = rank // size
    start = lax.axis_index("context") * share
    mine = [
        token_contract(lax.dynamic_slice_in_dim(b, start, share, 1), w)
        for b, w in zip(bases, omegas)
    ]
    summed = lax.psum(jnp.concatenate(mine, 0), "owner")
    whole = lax.all_gather(summed, "context", axis=0)
    whole = whole.reshape(size, len(bases), share, rank)
    return [whole[:, k].reshape(rank, rank) for k in range(len(bases))]


class Order:
    def __init__(self):
        self.last = ()

    def call(self, kernel, operands, out, after=(), vmem=8 * MIB, **rest):
        held = (*self.last, *after)
        count = len(operands)
        outs = out if isinstance(out, tuple) else (out,)
        steps = len(rest.get("grid", ()))

        def body(*refs):
            results = refs[count + len(held) :]
            mark = results[len(outs)]
            mark[...] = jnp.zeros_like(mark)
            kernel(*refs[:count], *results[: len(outs)], *results[len(outs) + 1 :])

        whole = pl.BlockSpec(memory_space=pltpu.VMEM)
        specs = rest.pop("in_specs", [whole] * count)
        out_specs = rest.pop("out_specs", [whole] * len(outs))
        zeros = (0, 0)
        marked = pl.BlockSpec((8, 128), lambda *_: zeros) if steps else whole
        *result, mark = pl.pallas_call(
            body,
            out_shape=(*outs, jax.ShapeDtypeStruct((8, 128), jnp.float32)),
            in_specs=[*specs, *[ANYWHERE] * len(held)],
            out_specs=[*out_specs, marked],
            cost_estimate=pl.CostEstimate(flops=10**9, bytes_accessed=10**7, transcendentals=0),
            compiler_params=pltpu.CompilerParams(vmem_limit_bytes=vmem),
            **rest,
        )(*operands, *held)
        self.last = (mark,)
        return tuple(result) if isinstance(out, tuple) else result[0]

    def gate(self, array, after=(), hbm=False):
        return self.call(
            lambda *_: None,
            (array,),
            pltpu.HBM(array.shape, array.dtype) if hbm else jax.ShapeDtypeStruct(array.shape, array.dtype),
            after,
            MIB,
            in_specs=[pl.BlockSpec(memory_space=pltpu.HBM) if hbm else ANYWHERE],
            out_specs=[pl.BlockSpec(memory_space=pltpu.HBM) if hbm else ANYWHERE],
            input_output_aliases={0: 0},
        )


def probe_rows(order, inputs, omega, start, rows, turned):
    depth, rank = omega.shape
    shape = jax.ShapeDtypeStruct((rows, rank), jnp.float32)
    tile = math.gcd(512, start, rows)
    first = start // tile

    def kernel(x, w, out):
        if turned:
            out[...] = token_contract(x[...], w[...])
        else:
            out[...] = jnp.dot(x[...], w[...], preferred_element_type=jnp.float32)

    if turned:
        spec = pl.BlockSpec((depth, tile), lambda i: (0, first + i))
    else:
        spec = pl.BlockSpec((tile, depth), lambda i: (first + i, 0))
    return order.call(
        kernel,
        (inputs, omega),
        shape,
        vmem=ROOM * MIB,
        grid=(rows // tile,),
        in_specs=[spec, pl.BlockSpec((depth, rank), lambda i: (0, 0))],
        out_specs=[pl.BlockSpec((tile, rank), lambda i: (i, 0))],
    )


def third(rows):
    return -(-rows // 24) * 8


def peaks(values):
    return jnp.maximum(jnp.max(jnp.abs(values), axis=1, keepdims=True), 1e-30)


def diagonal(rows, rank):
    shape = (rows, rank)
    return lax.broadcasted_iota(jnp.int32, shape, 0) == lax.broadcasted_iota(jnp.int32, shape, 1)


def pack(value, out, plain):
    group = third(plain)
    left = plain - 2 * group
    rank = value.shape[1]
    peak = peaks(value[:plain, :])
    scale = FINE / peak
    first = jnp.round(value[:group, :] * scale[:group])
    second = jnp.round(value[group : 2 * group, :] * scale[group : 2 * group])
    last = jnp.round(value[2 * group : plain, :] * (COARSE / peak[2 * group :]))
    high = jnp.round(last * (1 / 255))
    low = last - high * 255
    first, second = first * 256, second * 256
    out[:left, :] = first[:left] + high
    out[group : group + left, :] = second[:left] + low
    if left < group:
        out[left:group, :] = first[left:]
        out[group + left : 2 * group, :] = second[left:]
    out[2 * group : 2 * group + 8, :] = jnp.zeros((8, rank), jnp.float32)
    for k, start in enumerate(range(0, plain, rank)):
        part = peak[start : start + rank]
        row = jnp.where(diagonal(part.shape[0], rank), part, 0.0)
        out[2 * group + k : 2 * group + k + 1, :] = jnp.sum(row, axis=0, keepdims=True)
    if value.shape[0] > plain:
        out[2 * group + 8 :, :] = value[plain:, :]


def add_packed(mine, packed, plain):
    group = third(plain)
    left = plain - 2 * group
    rank = mine.shape[1]
    pieces = []
    for k, start in enumerate(range(0, plain, rank)):
        mask = diagonal(min(rank, plain - start), rank)
        row = jnp.where(mask, packed[2 * group + k : 2 * group + k + 1, :], 0.0)
        pieces.append(jnp.sum(row, axis=1, keepdims=True))
    peak = jnp.concatenate(pieces, 0)
    unit = peak * (1 / FINE)
    first, second = packed[:group, :], packed[group : 2 * group, :]
    whole = jnp.round(first * (1 / 256))
    high = first - whole * 256
    other = jnp.round(second * (1 / 256))
    low = second - other * 256
    last = high[:left] * 255 + low[:left]
    return (
        (0, group, mine[:group, :] + whole * unit[:group]),
        (group, 2 * group, mine[group : 2 * group, :] + other * unit[group : 2 * group]),
        (2 * group, plain, mine[2 * group : plain, :] + last * (peak[2 * group :] * (1 / COARSE))),
    )


def packed_shape(value, plain):
    rows = 2 * third(plain) + 8 + value.shape[0] - plain
    return jax.ShapeDtypeStruct((rows, value.shape[1]), jnp.float32)


def packed(order, partial, plain, after):
    shape = packed_shape(partial, plain)
    return order.call(lambda value, out: pack(value, out, plain), (partial,), shape, after)


def paired(order, partial, arrived, plain):
    def kernel(mine, theirs, out, message):
        for start, stop, rows in add_packed(mine, theirs, plain):
            out[start:stop, :] = rows
        if mine.shape[0] > plain:
            out[plain:, :] = mine[plain:, :] + theirs[2 * third(plain) + 8 :, :]
        pack(out, message, plain)

    shape = jax.ShapeDtypeStruct(partial.shape, jnp.float32)
    return order.call(kernel, (partial, arrived), (shape, packed_shape(partial, plain)))


def rounded(order, pair, arrived, plain, after):
    rows, rank = pair.shape
    exact = rows - plain

    def kernel(mine, theirs, out):
        for start, stop, total in add_packed(mine, theirs, plain):
            out[start:stop, :] = total.astype(jnp.bfloat16)
        if exact:
            rest = mine[plain:, :] + theirs[2 * third(plain) + 8 :, :]
            for i in range(TERMS):
                term = rest.astype(jnp.bfloat16)
                out[plain + i * exact : plain + (i + 1) * exact, :] = term
                rest = rest - term.astype(jnp.float32)

    shape = jax.ShapeDtypeStruct((plain + TERMS * exact, rank), jnp.bfloat16)
    return order.call(kernel, (pair, arrived), shape, after)


def pieces_of(chunks):
    if not isinstance(chunks, list):
        return [chunks], None
    parts = [array for own, received, _ in chunks for array in (own, received)]

    def fill(refs, probe):
        place = lax.axis_index("owner")
        inner = (place == 1) | (place == 2)
        start = 0
        for i, (_, _, rows) in enumerate(chunks):
            own, received = refs[2 * i], refs[2 * i + 1]
            probe[start : start + rows, :] = jnp.where(inner, own[:rows, :], received[:rows, :])
            start += rows

    return parts, fill


def data_half(order, inputs, chunks, half, before):
    features, tokens = inputs.shape
    parts, fill = pieces_of(chunks)
    rank = parts[0].shape[1]
    quarter = features // 4
    depth = tokens // SPLIT
    shape = pltpu.HBM((2, quarter, rank), jnp.float32)
    out_spec = pl.BlockSpec((1, quarter, rank), lambda i: (half, 0, 0))

    def kernel(x, p, *refs):
        given, kept, total = refs[-3:]
        odd = lax.axis_index("context") % 2 == 1
        step = pl.program_id(0)
        product = jnp.dot(x[...], p[...], preferred_element_type=jnp.float32)

        @pl.when(step == 0)
        def _():
            total[...] = product

        @pl.when(step > 0)
        def _():
            total[...] += product

        @pl.when((step == SPLIT - 1) & odd)
        def _():
            given[0] = total[:quarter, :]
            kept[0] = total[quarter:, :]

        @pl.when((step == SPLIT - 1) & jnp.logical_not(odd))
        def _():
            kept[0] = total[:quarter, :]
            given[0] = total[quarter:, :]

    return order.call(
        kernel,
        (inputs, *parts, *before),
        (shape, shape),
        vmem=ROOM * MIB,
        grid=(SPLIT,),
        in_specs=[
            pl.BlockSpec((2 * quarter, depth), lambda i: (half, i)),
            pl.BlockSpec((depth, rank), lambda i: (i, 0)),
            *[ANYWHERE] * len(before),
        ],
        out_specs=[out_spec, out_spec],
        scratch_shapes=[pltpu.VMEM((2 * quarter, rank), jnp.float32)],
        input_output_aliases={2: 0, 3: 1} if before else {},
    )


def data_parts(order, inputs, chunks, after):
    tokens = inputs.shape[0]
    parts, fill = pieces_of(chunks)
    rank = parts[0].shape[1]
    quarter = inputs.shape[1] // 4
    shape = jax.ShapeDtypeStruct((2, quarter, rank), jnp.float32)
    out_spec = pl.BlockSpec((1, quarter, rank), lambda i: (i, 0, 0))

    def kernel(x, *refs):
        given, kept, probe = refs[-3:] if fill else (*refs[-2:], refs[0])
        if fill:
            pl.when(pl.program_id(0) == 0)(lambda: fill(refs, probe))
        odd = lax.axis_index("context") % 2 == 1
        product = token_contract(x[...], probe[...])
        given[0] = jnp.where(odd, product[:quarter], product[quarter:])
        kept[0] = jnp.where(odd, product[quarter:], product[:quarter])

    return order.call(
        kernel,
        (inputs, *parts),
        (shape, shape),
        after,
        vmem=ROOM * MIB,
        grid=(2,),
        in_specs=[
            pl.BlockSpec((tokens, 2 * quarter), lambda i: (0, i)),
            *[pl.BlockSpec(p.shape, lambda i: (0, 0)) for p in parts],
        ],
        out_specs=[out_spec, out_spec],
        scratch_shapes=[pltpu.VMEM((tokens, rank), jnp.bfloat16)] if fill else [],
    )


def core_summed(order, kept, arrived):
    rows, rank = kept.shape[1:]

    def kernel(mine, theirs, stays, message, given):
        high = lax.select(lax.axis_index("context") >= 2, 1, 0)
        given[...] = mine[1 - high] + theirs[1 - high]
        stays[...] = mine[high] + theirs[high]
        pack(given, message, rows)

    shape = jax.ShapeDtypeStruct((rows, rank), jnp.float32)
    return order.call(
        kernel,
        (kept, arrived),
        (shape, packed_shape(shape, rows)),
        scratch_shapes=[pltpu.VMEM((rows, rank), jnp.float32)],
        vmem=(8 + rows // 96) * MIB,
    )


def finished(order, basis, eigen, cores, place, shares, scale):
    rows, rank = basis.shape
    part = cores.shape[0] // 4
    share = rank // 4

    def kernel(b, e, c, *refs):
        out = refs[-1]
        core = jnp.concatenate(
            [c[i * part + place * share : i * part + (place + 1) * share, :] for i in range(4)], 0
        )
        column = jnp.sum(jnp.where(diagonal(rank, rank), e[...], 0.0), axis=1, keepdims=True)
        rest = column * core
        prior = jnp.zeros((rows, rank), jnp.float32)
        for _ in range(3):
            term = rest.astype(jnp.bfloat16)
            prior += jnp.dot(b[...], term, preferred_element_type=jnp.float32)
            rest = rest - term.astype(jnp.float32)
        if len(refs) == 2:
            out[...] = 0.9 * prior + scale * refs[0][...]
        else:
            for start, stop, total in add_packed(refs[0], refs[1], rows):
                out[start:stop, :] = 0.9 * prior[start:stop] + scale * total

    shape = jax.ShapeDtypeStruct((rows, rank), jnp.float32)
    operands = (basis, eigen.reshape(1, rank), cores, *shares)
    return order.call(kernel, operands, shape, vmem=24 * MIB)


def core_parts(order, bases, omegas):
    rank = omegas[0].shape[1]
    share = rank // lax.axis_size("context")
    count = len(bases)

    def kernel(*refs):
        out, product = refs[-2:]
        start = pl.multiple_of(lax.axis_index("context") * share, share)
        for k in range(count):
            product[...] = token_contract(refs[k][...], refs[count + k][...])
            out[k * share : (k + 1) * share, :] = product[pl.ds(start, share), :]

    shape = jax.ShapeDtypeStruct((count * share, rank), jnp.float32)
    scratch = [pltpu.VMEM((rank, rank), jnp.float32)]
    return order.call(kernel, (*bases, *omegas), shape, vmem=ROOM * MIB, scratch_shapes=scratch)


def lines_of_four(inputs, omegas, bases, eigens, scale):
    turned = [x.shape[1] % 128 != 0 for x in inputs]
    inputs = [
        pltpu.with_memory_space_constraint(x.T if t else x, pltpu.HBM) if FENCED else x.T if t else x
        for x, t in zip(inputs, turned)
    ]
    order = Order()
    jobs = [k for k, _ in CHUNKS]
    count = len(jobs)
    partial, plain, message, inward, pair, across, probe, outward = (
        [None] * count for _ in range(8)
    )
    state = [None] * 3
    results = [None] * 3
    rank = omegas[0].shape[1]

    def multiply(i, after=()):
        k, share = CHUNKS[i]
        unit = inputs[k].shape[1 if turned[k] else 0] // 16
        start = unit * sum(n for j, n in CHUNKS[:i] if j == k)
        rows = unit * share
        partial[i] = probe_rows(order, inputs[k], omegas[k], start, rows, turned[k])
        if i == CARRIER:
            partial[i] = jnp.concatenate([partial[i], cores], 0)
        plain[i] = rows
        message[i] = packed(order, partial[i], rows, after)

    def send(i, after=()):
        if after:
            message[i] = order.gate(message[i], after)
        inward[i] = lax.ppermute(message[i], "owner", INWARD)

    def add_pair(i):
        pair[i], sums = paired(order, partial[i], inward[i], plain[i])
        across[i] = lax.ppermute(sums, "owner", ACROSS)

    def add_across(i, after=()):
        probe[i] = rounded(order, pair[i], across[i], plain[i], after)
        outward[i] = lax.ppermute(probe[i], "owner", OUTWARD)

    def carried(i):
        place = lax.axis_index("owner")
        inner = (place == 1) | (place == 2)
        terms = lax.select(inner, probe[i][plain[i] :], outward[i][plain[i] :])
        return jnp.sum(terms.reshape(TERMS, cores.shape[0], rank).astype(jnp.float32), 0)

    def probes(k):
        mine = [i for i in range(count) if jobs[i] == k]
        if not SELECTED:
            return [(probe[i], outward[i], plain[i]) for i in mine]
        place = lax.axis_index("owner")
        inner = (place == 1) | (place == 2)
        whole = [lax.select(inner, probe[i], outward[i])[: plain[i]] for i in mine]
        return jnp.concatenate(whole, 0)

    def contract(k, after=()):
        given, kept = data_parts(order, inputs[k], probes(k), after)
        state[k] = kept, given

    def share_out(k, now=False):
        kept, given = state[k]
        given = given if now else order.gate(given, (), turned[k])
        state[k] = kept, lax.ppermute(given, "context", PAIRED)

    def add_cores(k):
        stays, given = core_summed(order, *state[k])
        state[k] = stays, lax.ppermute(given, "context", SKIPPED)

    def finish(k):
        results[k] = finished(order, picked[k], eigens[k], whole, k, state[k], scale)

    def swapped(array, pairs, upper):
        theirs = lax.ppermute(order.gate(array), "context", pairs)
        return jnp.concatenate(
            [lax.select(upper, theirs, array), lax.select(upper, array, theirs)], 0
        )

    context = lax.axis_index("context")
    quarters = [b.shape[0] // 4 for b in bases]
    picked = [lax.dynamic_slice_in_dim(b, context * n, n, 0) for b, n in zip(bases, quarters)]
    halves = ()
    multiply(0)
    send(0)
    multiply(1)
    for i in range(count):
        for act in STEPS[i]:
            if act == "B":
                add_pair(i)
            elif act == "R":
                add_across(i - 1)
            else:
                send(i + 1, (inward[i],) if i < 2 else (inward[i], outward[i - 2]))
        if i == SWAPS[0]:
            pairs = swapped(totals, PAIRED, context % 2 == 1)
        if i == SWAPS[1]:
            whole = swapped(pairs, SKIPPED, context >= 2)
        if i == SHARED:
            share_out(2)
        if i == CARRIER - 2:
            cores = core_parts(order, bases, omegas)
        if i + 2 < count:
            multiply(i + 2, picked if i == 0 else ())
        if i in PIECES:
            halves = data_half(order, inputs[2], probes(2), PIECES.index(i), halves)
            state[2] = halves[1], halves[0]
        if i == ATTN:
            contract(0, (whole,) if WAITS == 2 else ())
        if i == CARRIER + 1:
            totals = carried(CARRIER)
        if i == 5:
            share_out(0)
        if i == SUMMED:
            add_cores(2)
        if i == 5:
            add_cores(0)
    add_across(count - 1)
    if EARLY == 1:
        finish(2)
    contract(1, (whole,) if WAITS == 1 else ())
    share_out(1, True)
    if EARLY == 2:
        finish(2)
    add_cores(1)
    if EARLY == 0:
        finish(2)
    finish(0)
    finish(1)
    return tuple(results)


def any_lines(inputs, omegas, bases, eigens, scale):
    cores = core_total(bases, omegas)
    results = []
    for x, w, b, e, core in zip(inputs, omegas, bases, eigens, cores):
        partial = jnp.dot(x, w, preferred_element_type=jnp.float32)
        share = lax.psum_scatter(partial, "owner", scatter_dimension=0, tiled=True)
        probe = lax.all_gather(share.astype(jnp.bfloat16), "owner", axis=0, tiled=True)
        data = lax.psum_scatter(
            token_contract(x, probe), "context", scatter_dimension=0, tiled=True
        )
        results.append(prior_rows(b, e, core) + scale * data)
    return tuple(results)


def per_device(
    x_attn,
    x_mlp,
    x_down,
    omega_attn,
    omega_mlp,
    omega_down,
    basis_attn,
    basis_mlp,
    basis_down,
    eig_attn,
    eig_mlp,
    eig_down,
):
    inputs = (x_attn, x_mlp, x_down)
    omegas = (omega_attn, omega_mlp, omega_down)
    bases = (basis_attn, basis_mlp, basis_down)
    eigens = (eig_attn, eig_mlp, eig_down)
    scale = 0.1 / (x_attn.shape[0] * lax.axis_size("context"))
    fours = lax.axis_size("owner") == 4 and lax.axis_size("context") == 4
    run = lines_of_four if fours else any_lines
    return run(inputs, omegas, bases, eigens, scale)


def solution(mesh):
    placed = (
        P(("section", "context"), "owner"),
        P(("section", "context"), "owner"),
        P(("section", "context"), "owner"),
        P(("section", "owner"), None),
        P(("section", "owner"), None),
        P(("section", "owner"), None),
        P(("section", "owner"), None),
        P(("section", "owner"), None),
        P(("section", "owner"), None),
        P("section"),
        P("section"),
        P("section"),
    )
    return jax.shard_map(
        per_device,
        mesh=mesh,
        in_specs=placed,
        out_specs=(
            P(("section", "owner", "context"), None),
            P(("section", "owner", "context"), None),
            P(("section", "owner", "context"), None),
        ),
        check_vma=False,
    )
```
